32 devices in a mesh: cell: 2 (over x), blk: 16 (over z, y, core).
Axes of the slice: x: 2, y: 2, z: 4, core: 2. Of those that a mesh axis runs over, the one named last changes fastest.
Arguments:
- psi_val: float32 [256, 64, 64, 64], P('cell', 'blk'), parts along dimension 0, may hold values from -6 to 6
- psi_cond: float32 [6, 64, 64, 64], P('cell', 'blk'), parts along dimension 0, may hold values from -6 to 6
- e_val: float32 [256], P('cell'), parts along dimension 0, may hold values from -8 to -1
- e_cond: float32 [6], P('cell'), parts along dimension 0, may hold values from 1 to 8
- occ: int32 [256], P('cell'), parts along dimension 0, may hold values from 1 to 2
- freq: float32 [10], P('cell'), parts along dimension 0, may hold values from 0.5 to 16
- gmap: int32 [8192], P('cell'), parts along dimension 0, may hold values from 0 to 262143, as said below
Outputs:
- chi_real: float32 [10, 4096, 4096], P('cell', 'blk'), parts along dimension 0
- chi_imag: float32 [10, 4096, 4096], P('cell', 'blk'), parts along dimension 0
The draws below stay inside these ranges and needn't reach their ends.
There are 2 independent parts, one for each index of `cell`. The reference program is written for one: setup_inputs(seed, part) draws one part's arguments, and reference() takes and returns one part's arrays. A program takes and returns all parts, laid end to end along the dimension named above; each array names one. Nothing has to cross between parts.
Inputs may be any that keep to these rules, and one draw needn't show every extreme that they name: `gmap`: the 4096 indices are distinct; index 0 and index 262143 are always among them.
All inputs are finite; a program needn't handle non-finite values.
Results may differ from the reference program's by a relative error of at most 0.0001.
Values sent between devices are 32-bit elements; how exact they have to be, the bound alone decides.
A program may use at most 256 MiB of HBM per device.

```python
import math
import jax
import jax.numpy as jnp
from jax import lax

GX = 64
GY = 64
GZ = 64
NG = 4096
VAL = 128
COND = 3
NFREQ = 5


def draw_gmap(key, part):
    total_points = GX * GY * GZ
    inner = jax.random.permutation(jax.random.fold_in(key, 11), total_points - 2)[:NG - 2] + 1
    ends = jnp.array([0, total_points - 1], dtype=jnp.int32)
    joined = jnp.concatenate([inner.astype(jnp.int32), ends])
    return jax.random.permutation(jax.random.fold_in(key, 23), joined).astype(jnp.int32)


def plant(drawn, stream_key, least, high):
    longest = drawn.shape.index(max(drawn.shape))
    spots = []
    for shift in (0, 1):
        where = [jax.random.randint(jax.random.fold_in(stream_key, axis), (), 0, length) for axis, length in enumerate(drawn.shape)]
        where[longest] = (where[longest] + shift) % drawn.shape[longest]
        spots.append(tuple(where))
    return drawn.at[spots[0]].set(least).at[spots[1]].set(high)


def block_scale(own_key, extent, cuts, smallest, largest):
    def one(position, shards_of):
        heights = jax.random.uniform(jax.random.fold_in(jax.random.fold_in(own_key, 6), position), (shards_of,), jnp.float32, smallest / len(cuts), largest / len(cuts))
        return jnp.repeat(jnp.exp(heights), extent[position] // shards_of).reshape((-1,) + (1,) * (len(extent) - position - 1))

    gain = one(*cuts[0])
    for cut in cuts[1:]:
        gain = gain * one(*cut)
    return gain


def scatter_about(own_key, shape, deviation, most, pieces=(), held_as=jnp.bfloat16):
    drawn = jax.random.normal(own_key, shape, jnp.float32) * deviation
    if len(pieces) > 0:
        drawn = block_scale(own_key, shape, pieces, -0.22, 0.18) * drawn
    return jnp.clip(drawn, min=-most, max=most).astype(held_as)


def setup_inputs(seed: int = 0, part: int = 0) -> dict:
    streams_of = jax.random.split(jax.random.key(seed), 8)
    own_keys = jax.random.split(jax.random.fold_in(streams_of[7], part), 8)
    psi_val = scatter_about(own_keys[0], (VAL, GX, GY, GZ), 1.0, 6.0, ((1, 16),), jnp.float32)
    psi_cond = scatter_about(own_keys[1], (COND, GX, GY, GZ), 1.0, 6.0, ((1, 16),), jnp.float32)
    e_val = jnp.clip(jax.random.uniform(own_keys[2], (VAL,), jnp.float32, -8.0, -1.0), -8.0, -1.0)
    e_cond = jnp.clip(jax.random.uniform(own_keys[3], (COND,), jnp.float32, 1.0, 8.0), 1.0, 8.0)
    occ = plant(jax.random.randint(own_keys[4], (VAL,), 1, 3), jax.random.fold_in(own_keys[4], 1), 1, 2).astype(jnp.int32)
    freq = jnp.clip(jnp.exp(jax.random.uniform(own_keys[5], (NFREQ,), jnp.float32, math.log(0.5), math.log(16.0))), 0.5, 16.0)
    gmap = draw_gmap(jax.random.fold_in(jax.random.fold_in(streams_of[7], part), 71), part)
    return {"psi_val": psi_val, "psi_cond": psi_cond, "e_val": e_val, "e_cond": e_cond, "occ": occ, "freq": freq, "gmap": gmap}


def reference(psi_val, psi_cond, e_val, e_cond, occ, freq, gmap):
    total_points = GX * GY * GZ
    norm_factor = 1.0 / math.sqrt(total_points)

    def one_band(band):
        density = psi_val[band][None] * psi_cond
        spectrum = jnp.fft.fftn(density, axes=(1, 2, 3)).reshape(COND, total_points)
        picked = jnp.take(spectrum, gmap, axis=1)
        return (picked.real * norm_factor, picked.imag * norm_factor)
    real_m, imag_m = lax.map(one_band, jnp.arange(VAL, dtype=jnp.int32))
    real_m = real_m.reshape(VAL * COND, NG)
    imag_m = imag_m.reshape(VAL * COND, NG)
    gaps = (e_val[:, None] - e_cond[None, :]).reshape(VAL * COND)
    occ_pairs = jnp.broadcast_to(occ.astype(jnp.float32)[:, None], (VAL, COND)).reshape(VAL * COND)
    stacked = jnp.concatenate([real_m, imag_m], axis=0)
    real_list = []
    imag_list = []
    for step in range(NFREQ):
        weights = occ_pairs * gaps / (gaps * gaps + freq[step] * freq[step])
        weights = weights / math.sqrt(VAL * COND)
        left_real = jnp.concatenate([weights[:, None] * real_m, weights[:, None] * imag_m], axis=0)
        left_imag = jnp.concatenate([weights[:, None] * imag_m, -weights[:, None] * real_m], axis=0)
        real_list.append(jnp.dot(left_real.T, stacked, precision=lax.Precision.HIGHEST, preferred_element_type=jnp.float32))
        imag_list.append(jnp.dot(left_imag.T, stacked, precision=lax.Precision.HIGHEST, preferred_element_type=jnp.float32))
    return (jnp.stack(real_list), jnp.stack(imag_list))
```

```python
import math

import jax
import jax.numpy as jnp
from jax import lax
from jax.sharding import PartitionSpec as P

high = lax.Precision.HIGH


def dft_tables(rows, length):
    angles = (
        jnp.arange(rows, dtype=jnp.int32)[:, None]
        * jnp.arange(length, dtype=jnp.int32)[None, :]
        % length
    ).astype(jnp.float32) * (2.0 * math.pi / length)
    return (jnp.cos(angles), jnp.sin(angles))


def plane_transform(val_part, cond_part):
    num_val, planes, size_y, size_z = val_part.shape
    num_cond = cond_part.shape[0]
    half = size_z // 2 + 1
    val_t = jnp.transpose(val_part, (1, 3, 2, 0))
    cond_t = jnp.transpose(cond_part, (1, 0, 3, 2))
    density = jnp.concatenate(
        [
            val_t[x] * cond_t[x, c][:, :, None]
            for x in range(planes)
            for c in range(num_cond)
        ],
        axis=2,
    )
    columns = planes * num_cond * num_val
    cos_z, sin_z = dft_tables(half, size_z)
    table_z = jnp.stack([cos_z, -sin_z], axis=1).reshape(2 * half, size_z)
    after_z = jnp.einsum("mz,zyn->myn", table_z, density, precision=high)
    after_z = after_z.reshape(half, 2 * size_y, columns)
    cos_y, sin_y = dft_tables(size_y, size_y)
    table_y = jnp.concatenate(
        [
            jnp.concatenate([cos_y, sin_y], axis=1),
            jnp.concatenate([-sin_y, cos_y], axis=1),
        ],
        axis=0,
    )
    after_y = jnp.einsum("rs,ksn->krn", table_y, after_z, precision=high)
    return after_y.reshape(half * 2 * size_y, columns)


def body(psi_val, psi_cond, e_val, e_cond, occ, freq, gmap):
    num_val, planes, size_y, size_z = psi_val.shape
    num_cond = psi_cond.shape[0]
    pairs = num_val * num_cond
    size_x = planes * lax.axis_size("blk")
    norm_factor = 1.0 / math.sqrt(size_x * size_y * size_z)

    kx = gmap // (size_y * size_z)
    ky = gmap // size_z % size_y
    kz = gmap % size_z
    mirrored = kz > size_z // 2
    row = jnp.where(
        mirrored,
        (size_z - kz) * 2 * size_y + (size_y - ky) % size_y,
        kz * 2 * size_y + ky,
    )
    sign = jnp.where(mirrored, -1.0, 1.0).astype(jnp.float32)[:, None]
    spectrum = plane_transform(psi_val, psi_cond)
    real_v = spectrum.at[row].get(mode="promise_in_bounds")
    imag_v = spectrum.at[row + size_y].get(mode="promise_in_bounds")

    positions = lax.axis_index("blk") * planes + jnp.arange(planes, dtype=jnp.int32)
    angles = (kx[:, None] * positions[None, :] % size_x).astype(jnp.float32) * (
        2.0 * math.pi / size_x
    )
    cosine = jnp.cos(angles) * norm_factor
    sine = jnp.sin(angles) * norm_factor
    real_m = 0.0
    imag_m = 0.0
    for x in range(planes):
        real_x = real_v[:, x * pairs : (x + 1) * pairs]
        imag_x = imag_v[:, x * pairs : (x + 1) * pairs] * sign
        real_m = real_m + real_x * cosine[:, x : x + 1] + imag_x * sine[:, x : x + 1]
        imag_m = imag_m + imag_x * cosine[:, x : x + 1] - real_x * sine[:, x : x + 1]
    owned = lax.psum_scatter(
        jnp.concatenate([real_m, imag_m], axis=1), "blk", scatter_dimension=0, tiled=True
    )
    everyone = lax.all_gather(owned, "blk", axis=0, tiled=True)

    gaps = (e_val[None, :] - e_cond[:, None])[:, :, None]
    weights = (
        occ.astype(jnp.float32)[None, :, None] * gaps / (gaps * gaps + (freq * freq)[None, None, :])
    )
    weights = weights.reshape(pairs, freq.shape[0]) / math.sqrt(pairs)
    freq_weights = jnp.transpose(weights)[:, None, :]
    real_w = owned[None, :, :pairs] * freq_weights
    imag_w = owned[None, :, pairs:] * freq_weights
    chi_real = jnp.einsum(
        "wgk,hk->wgh", jnp.concatenate([real_w, imag_w], axis=2), everyone, precision=high
    )
    chi_imag = jnp.einsum(
        "wgk,hk->wgh", jnp.concatenate([imag_w, -real_w], axis=2), everyone, precision=high
    )
    return (chi_real, chi_imag)


def solution(mesh):
    return jax.shard_map(
        body,
        mesh=mesh,
        in_specs=(
            P("cell", "blk", None, None),
            P("cell", "blk", None, None),
            P("cell"),
            P("cell"),
            P("cell"),
            P("cell"),
            P("cell"),
        ),
        out_specs=(P("cell", "blk", None), P("cell", "blk", None)),
        check_vma=False,
    )
```
